32 devices in a mesh: pipe: 4 (over y, core), ctx: 4 (over z), width: 2 (over x).
Axes of the slice: x: 2, y: 2, z: 4, core: 2. Of those that a mesh axis runs over, the one named last changes fastest.
Arguments:
- tokens: int32 [512], P('ctx'), may hold values from 0 to 511
- table: bfloat16 [512, 8192], P(None, 'width'), may hold values from -6 to 6
- boundary: bfloat16 [4, 2, 512, 8192], P('pipe', None, 'ctx', 'width'), may hold values from -24 to 24, as said below
- saved_in: bfloat16 [4, 512, 8192], P('pipe', 'ctx', 'width'), may hold values from -24 to 24, as said below
- loss_grad: bfloat16 [512, 8192], P('ctx', 'width'), may hold values from -6 to 6
- gain: float32 [4, 8192], P('pipe', 'width'), may hold values from 0.1 to 1.9
- skip: float32 [4, 8192], P('pipe', 'width'), may hold values from -4 to 4
- residue: float32 [4, 16, 8192], P('pipe', None, 'width'), may hold values from -1.5 to 1.5
- decay_rate: float32 [4, 16, 8192], P('pipe', None, 'width'), may hold values from 0.000390625 to 2, as said below
Outputs:
- segment_out: bfloat16 [4, 512, 8192], P('pipe', 'ctx', 'width')
- input_grad: bfloat16 [4, 512, 8192], P('pipe', 'ctx', 'width')
- gain_grad: float32 [4, 4, 8192], P('pipe', 'ctx', 'width')
- skip_grad: float32 [4, 4, 8192], P('pipe', 'ctx', 'width')
The draws below stay inside these ranges and needn't reach their ends.
Inputs may be any that keep to these rules, and one draw needn't show every extreme that they name: `boundary`: activations and gradients stored from earlier steps. `saved_in`: a stored input. `decay_rate`: positive decays.
All inputs are finite; a program needn't handle non-finite values.
Results may differ from the reference program's by a relative error of at most 0.0034.
Values may be sent and summed in bfloat16 or wider, within the bound.
A program may use at most 128 MiB of HBM per device.

```python
import math
import jax
import jax.numpy as jnp
import numpy as np
from jax import lax

D = 8192
VOCAB = 512
ORDER = 16
BLK = 16
L_DEV = 128
SEQ = 512
N_PIPE = 4
N_CTX = 4


def draw_activity(key, full_shape):
    base_key, row_key, col_key = jax.random.split(key, 3)
    base_draw = jnp.clip(jax.random.normal(base_key, full_shape, jnp.float32), -3.0, 3.0)
    row_scale = jnp.exp(jax.random.uniform(row_key, full_shape[:-1] + (1,), jnp.float32, -0.693, 0.693))
    col_scale = jnp.exp(1.0986 * jnp.arange(D, dtype=jnp.float32) / D + jax.random.uniform(col_key, (D,), jnp.float32, -0.693, 0.693))
    return jnp.clip(base_draw * row_scale * col_scale, -24.0, 24.0)


def draw_boundary(key, part):
    return draw_activity(jax.random.fold_in(key, 11), (N_PIPE, 2, SEQ, D)).astype(jnp.bfloat16)


def draw_saved_in(key, part):
    return draw_activity(jax.random.fold_in(key, 12), (N_PIPE, SEQ, D)).astype(jnp.bfloat16)


def draw_decay_rate(key, part):
    slow_key, fast_key, pick_key = jax.random.split(jax.random.fold_in(key, 13), 3)
    full_shape = (N_PIPE, ORDER, D)
    slow_rates = jnp.exp(jax.random.uniform(slow_key, full_shape, jnp.float32, jnp.log(0.2 / SEQ), jnp.log(2.0 / SEQ)))
    fast_rates = jnp.exp(jax.random.uniform(fast_key, full_shape, jnp.float32, jnp.log(1.0 / 50.0), jnp.log(2.0)))
    slow_share = 0.5
    chosen = jax.random.uniform(pick_key, full_shape, jnp.float32) < slow_share
    return jnp.where(chosen, slow_rates, fast_rates)


def with_ends(drawn, key, smallest, high):
    index_at = [jax.random.randint(jax.random.fold_in(key, axis), (), 0, length) for axis, length in enumerate(drawn.shape)]
    longest = drawn.shape.index(max(drawn.shape))
    next_to = index_at[:longest] + [(index_at[longest] + 1) % drawn.shape[longest]] + index_at[longest + 1:]
    return drawn.at[tuple(index_at)].set(smallest).at[tuple(next_to)].set(high)


def levels(stream_key, shape, cuts, low, top_value):
    loudness, own = 1.0, jax.random.fold_in(stream_key, 6)
    for axis_at, parts in cuts:
        steps = jnp.exp(jax.random.uniform(jax.random.fold_in(own, axis_at), (parts,), jnp.float32, low / len(cuts), top_value / len(cuts)))
        loudness = loudness * jnp.repeat(steps, shape[axis_at] // parts).reshape([-1 if axis == axis_at else 1 for axis in range(len(shape))])
    return loudness


def cumulative_ranks(count, slope):
    loads = [(1 << 20) // math.isqrt(standing ** slope) + 1 for standing in range(1, count + 1)]
    deviation = 1 + sum(loads) // (1 << 30)
    return np.cumsum(np.array([max(1, weight // deviation) for weight in loads]))


def skewed_ids(key, dims, amount, lean):
    listing = cumulative_ranks(amount, lean)
    pick = jax.random.randint(jax.random.fold_in(key, 1), dims, 0, int(listing[amount - 1]))
    standing = jnp.searchsorted(jnp.asarray(listing, jnp.int32), pick, side="right")
    return jax.random.permutation(jax.random.fold_in(key, 2), amount)[standing].astype(jnp.int32)


def gaussian(rng, dims, deviation, reach, cuts=(), kind=jnp.bfloat16):
    values = deviation * jax.random.normal(rng, dims, jnp.float32)
    if cuts:
        values = values * levels(rng, dims, cuts, -0.22, 0.18)
    return jnp.clip(values, -reach, reach).astype(kind)


def setup_inputs(seed: int = 0) -> dict:
    streams_of = jax.random.split(jax.random.key(seed), 10)
    tokens = with_ends(skewed_ids(streams_of[0], (SEQ,), VOCAB, 2), jax.random.fold_in(streams_of[0], 3), 0, VOCAB - 1).astype(jnp.int32)
    table = gaussian(streams_of[1], (VOCAB, D), 1.0, 6.0, ((1, 2),))
    boundary = draw_boundary(jax.random.fold_in(streams_of[9], 71), 0)
    saved_in = draw_saved_in(jax.random.fold_in(streams_of[9], 71), 0)
    loss_grad = gaussian(streams_of[4], (SEQ, D), 1.0, 6.0, ((0, 4), (1, 2)))
    gain = jnp.clip(1.0 + 0.18 * jax.random.normal(streams_of[5], (N_PIPE, D), jnp.float32), 0.1, 1.9)
    skip = gaussian(streams_of[6], (N_PIPE, D), 1.0, 4.0, ((0, 4), (1, 2)), jnp.float32)
    residue = gaussian(streams_of[7], (N_PIPE, ORDER, D), ORDER ** -0.5, 1.5, ((0, 4), (2, 2)), jnp.float32)
    decay_rate = draw_decay_rate(jax.random.fold_in(streams_of[9], 71), 0)
    return {"tokens": tokens, "table": table, "boundary": boundary, "saved_in": saved_in, "loss_grad": loss_grad, "gain": gain, "skip": skip, "residue": residue, "decay_rate": decay_rate}


epsilon = 1e-06

def conv_tables(damping, scaled_residue, block_len):
    lags = jnp.arange(block_len, dtype=jnp.float32)
    decay_pow = jnp.exp(-damping[:, None, :] * lags[None, :, None])
    kernel = lax.optimization_barrier(jnp.sum(scaled_residue[:, None, :] * decay_pow, axis=0))
    diff_index = np.maximum(np.arange(block_len)[:, None] - np.arange(block_len)[None, :], 0)
    lower_mask = (np.arange(block_len)[:, None] >= np.arange(block_len)[None, :]).astype(np.float32)
    toeplitz = kernel[diff_index.reshape(-1)].reshape(block_len, block_len, -1) * jnp.asarray(lower_mask)[:, :, None]
    tail = jnp.flip(decay_pow, 1)
    lead = scaled_residue[:, None, :] * decay_pow * jnp.exp(-damping)[:, None, :]
    stride = jnp.exp(-damping * float(block_len))
    return (toeplitz, tail, lead, stride)

def local_conv(signal, tables):
    toeplitz, tail, lead, stride = tables
    length, channels = signal.shape
    block_len = toeplitz.shape[0]
    pieces = signal.reshape(length // block_len, block_len, channels)
    output = jnp.einsum('ijc,bjc->bic', toeplitz, pieces, precision=lax.Precision.HIGHEST)
    summary = jnp.einsum('kjc,bjc->bkc', tail, pieces, precision=lax.Precision.HIGHEST)

    def advance(state_now, block_sum):
        return (stride * state_now + block_sum, state_now)
    last_state, entries = lax.scan(advance, jnp.zeros(stride.shape, jnp.float32), summary)
    return (output, entries, last_state)

def finish_conv(output, entries, tables):
    toeplitz, tail, lead, stride = tables
    carried = jnp.einsum('kic,bkc->bic', lead, entries, precision=lax.Precision.HIGHEST)
    total = output + carried
    return total.reshape(total.shape[0] * total.shape[1], total.shape[2])

def segment_step(incoming, cotangent_in, saved, gain_row, skip_row, residue_row, damping):
    scaled_residue = residue_row * jnp.sqrt(1.0 - jnp.exp(-2.0 * damping))
    tables = conv_tables(damping, scaled_residue, BLK)
    forward_in = incoming.astype(jnp.float32)
    saved_rows = saved.astype(jnp.float32)
    scale_fwd = lax.rsqrt(lax.optimization_barrier(jnp.sum(forward_in * forward_in, axis=1, keepdims=True)) / D + epsilon)
    scale_back = lax.rsqrt(lax.optimization_barrier(jnp.sum(saved_rows * saved_rows, axis=1, keepdims=True)) / D + epsilon)
    normed_fwd = forward_in * scale_fwd * gain_row
    normed_back = saved_rows * scale_back * gain_row
    out_fwd, ent_fwd, unused_fwd = local_conv(normed_fwd, tables)
    out_back, ent_back, unused_back = local_conv(normed_back, tables)
    mixed_fwd = finish_conv(out_fwd, ent_fwd, tables) + skip_row * normed_fwd
    mixed_back = finish_conv(out_back, ent_back, tables) + skip_row * normed_back
    segment_out = (forward_in + normed_fwd * mixed_fwd).astype(jnp.bfloat16)
    cotangent = cotangent_in.astype(jnp.float32)
    grad_mix = cotangent * normed_back
    out_rev, ent_rev, unused_rev = local_conv(jnp.flip(grad_mix, 0), tables)
    back_term = jnp.flip(finish_conv(out_rev, ent_rev, tables), 0)
    grad_norm = cotangent * mixed_back + skip_row * grad_mix + back_term
    grad_scaled = grad_norm * gain_row
    inner_sum = lax.optimization_barrier(jnp.sum(grad_scaled * saved_rows, axis=1, keepdims=True))
    input_grad = (cotangent + scale_back * grad_scaled - saved_rows * scale_back ** 3 * inner_sum / D).astype(jnp.bfloat16)
    gain_grad = lax.optimization_barrier(jnp.sum((grad_norm * saved_rows * scale_back).reshape(N_CTX, L_DEV, D), axis=1))
    skip_grad = lax.optimization_barrier(jnp.sum((grad_mix * normed_back).reshape(N_CTX, L_DEV, D), axis=1))
    return (segment_out, input_grad, gain_grad, skip_grad)

def reference(tokens, table, boundary, saved_in, loss_grad, gain, skip, residue, decay_rate):
    embedded = jnp.take(table, tokens, axis=0)
    incoming = jnp.concatenate([embedded[None], boundary[:-1, 1]], axis=0)
    cotangent = jnp.concatenate([boundary[1:, 0], loss_grad[None]], axis=0)

    def one_segment(bundle):
        return segment_step(bundle[0], bundle[1], bundle[2], bundle[3], bundle[4], bundle[5], bundle[6])
    results = lax.map(one_segment, (incoming, cotangent, saved_in, gain, skip, residue, decay_rate))
    return (results[0], results[1], results[2], results[3])
```

```python
import jax
import jax.numpy as jnp
from jax import lax
from jax.experimental import pallas as pl
from jax.experimental.pallas import tpu as pltpu
from jax.sharding import PartitionSpec as P

D = 8192
ROWS = 8
LANES = 128
CHUNK = 512
epsilon = 1e-06


def shifted(value, axis, steps):
    count = lax.axis_size(axis)
    initial, last = (max(0, -steps), min(count, count - steps))
    return lax.ppermute(value, axis, [(source, source + steps) for source in range(initial, last)])


def width_sum(value):
    if lax.axis_size("width") == 2:
        return value + lax.ppermute(value, "width", [(0, 1), (1, 0)])
    return lax.psum(value, "width")


def wide(row):
    return jnp.broadcast_to(row, (ROWS, LANES))


def states_kernel(x_ref, sav_ref, cot_ref, sf_ref, sb_ref, gain_ref, decay_ref,
                  e_ref, end_ref, sig, last):
    length = x_ref.shape[0]
    steps = length // ROWS
    modes = decay_ref.shape[0]
    place = lax.broadcasted_iota(jnp.int32, (ROWS, LANES), 0)

    def group(g, carry):
        lanes = pl.ds(pl.multiple_of(g * LANES, LANES), LANES)
        gain = gain_ref[:, lanes]
        back = sav_ref[:, lanes].astype(jnp.float32) * sb_ref[...] * gain
        sig[0] = x_ref[:, lanes].astype(jnp.float32) * sf_ref[...] * gain
        sig[1] = back
        sig[2] = cot_ref[:, lanes].astype(jnp.float32) * back
        damping = decay_ref[:, lanes]
        a_all = jnp.exp(-damping)
        stride_all = jnp.exp(-damping * float(steps))
        a = [wide(a_all[k:k + 1]) for k in range(modes)]
        for q in range(3):
            rev = q == 2
            order = range(steps - 1, -1, -1) if rev else range(steps)
            state = None
            for j in order:
                piece = sig[q, pl.ds(j, ROWS, stride=steps), :]
                if state is None:
                    state = [piece] * modes
                else:
                    state = [a[k] * state[k] + piece for k in range(modes)]
            for k in range(modes):
                power = wide(stride_all[k:k + 1])
                total = state[k]
                hop = 1
                while hop < ROWS:
                    near = (place < ROWS - hop) if rev else (place >= hop)
                    moved = pltpu.roll(total, ROWS - hop if rev else hop, 0)
                    total = total + jnp.where(near, power * moved, 0.0)
                    power = power * power
                    hop *= 2
                near = (place < ROWS - 1) if rev else (place >= 1)
                moved = pltpu.roll(total, ROWS - 1 if rev else 1, 0)
                e_ref[q, k, :, lanes] = jnp.where(near, moved, 0.0)
                edge = 0 if rev else ROWS - 1
                last[k:k + 1, :] = total[edge:edge + 1, :]
            end_ref[q, :, lanes] = last[...].astype(end_ref.dtype)
        return carry

    lax.fori_loop(0, x_ref.shape[1] // LANES, group, 0)


def finish_kernel(mine_ref, x_ref, sav_ref, cot_ref, sf_ref, sb_ref, gain_ref, skip_ref,
                  residue_ref, decay_ref, e_ref, ends_ref,
                  out_ref, part_ref, gg_ref, sg_ref, acc_ref, sig, res):
    length = x_ref.shape[0]
    steps = length // ROWS
    modes = decay_ref.shape[0]
    peers = ends_ref.shape[0]
    mine = mine_ref[0]
    place = lax.broadcasted_iota(jnp.int32, (ROWS, LANES), 0).astype(jnp.float32)

    @pl.when(pl.program_id(0) == 0)
    def _():
        acc_ref[...] = jnp.zeros_like(acc_ref)

    def group(g, carry):
        lanes = pl.ds(pl.multiple_of(g * LANES, LANES), LANES)
        gain = gain_ref[:, lanes]
        gain_w = wide(gain)
        sig[0] = x_ref[:, lanes].astype(jnp.float32)
        sig[1] = sav_ref[:, lanes].astype(jnp.float32) * sb_ref[...]
        sig[2] = cot_ref[:, lanes].astype(jnp.float32)
        damping = decay_ref[:, lanes]
        a_all = jnp.exp(-damping)
        coefs = residue_ref[:, lanes] * jnp.sqrt(1.0 - jnp.exp(-2.0 * damping))
        whole = jnp.exp(-damping * float(length))
        entering = []
        for q in range(3):
            total = jnp.zeros((modes, LANES), jnp.float32)
            for hop in range(peers - 1):
                at = peers - 1 - hop if q == 2 else hop
                reached = (at > mine) if q == 2 else (at < mine)
                longer = whole * total + ends_ref[at, q, :, lanes].astype(jnp.float32)
                total = jnp.where(reached, longer, total)
            entering.append(total)
        kernel = []
        power = coefs
        for n in range(steps):
            kernel.append(wide(jnp.sum(power, axis=0, keepdims=True)))
            power = power * a_all
        kernel[0] = kernel[0] + wide(skip_ref[:, lanes])

        def rows(i):
            return pl.ds(i, ROWS, stride=steps)

        def conv(q, pieces, emit):
            rev = q == 2
            ago = (float(ROWS - 1) - place) if rev else place
            decayed = []
            for k in range(modes):
                gap = jnp.exp(wide(damping[k:k + 1]) * (ago * float(-steps)))
                state = e_ref[q, k, :, lanes] + gap * wide(entering[q][k:k + 1])
                decayed.append(wide(coefs[k:k + 1]) * state)
            a = [wide(a_all[k:k + 1]) for k in range(modes)]
            for n in range(steps):
                decayed = [a[k] * decayed[k] for k in range(modes)]
                terms = decayed + [kernel[n - m] * pieces[steps - 1 - m if rev else m]
                                   for m in range(n + 1)]
                sums = terms[:4]
                for index, term in enumerate(terms[4:]):
                    sums[index % 4] = sums[index % 4] + term
                emit(steps - 1 - n if rev else n, (sums[0] + sums[1]) + (sums[2] + sums[3]))

        raw = [sig[0, rows(i), :] for i in range(steps)]
        normed = [raw[i] * sf_ref[rows(i), :] * gain_w for i in range(steps)]

        def emit_out(i, value):
            res[0, rows(i), :] = sig[0, rows(i), :] + sig[0, rows(i), :] * sf_ref[rows(i), :] * gain_w * value

        conv(0, normed, emit_out)
        out_ref[:, lanes] = res[0].astype(out_ref.dtype)

        back = [sig[1, rows(i), :] * gain_w for i in range(steps)]

        def emit_mixed(i, value):
            res[1, rows(i), :] = sig[2, rows(i), :] * value

        conv(1, back, emit_mixed)

        mix = [sig[2, rows(i), :] * back[i] for i in range(steps)]
        skip_sum = mix[0] * back[0]
        for i in range(1, steps):
            skip_sum = skip_sum + mix[i] * back[i]
        sg_ref[:, lanes] = jnp.sum(skip_sum, axis=0, keepdims=True)
        gain_sums = [jnp.zeros((ROWS, LANES), jnp.float32)]

        def emit_grad(i, value):
            norm = res[1, rows(i), :] + value
            unit = sig[1, rows(i), :]
            gain_sums[0] = gain_sums[0] + norm * unit
            scaled = gain_w * norm
            acc_ref[i] = acc_ref[i] + scaled * unit
            res[2, rows(i), :] = sig[2, rows(i), :] + sb_ref[rows(i), :] * scaled

        conv(2, mix, emit_grad)
        part_ref[:, lanes] = res[2]
        gg_ref[:, lanes] = jnp.sum(gain_sums[0], axis=0, keepdims=True)
        return carry

    lax.fori_loop(0, x_ref.shape[1] // LANES, group, 0)


def local(tokens, table, boundary, saved_in, loss_grad, gain, skip, residue, decay_rate):
    segment_index = lax.axis_index("pipe")
    segments = lax.axis_size("pipe")
    arrived = shifted(boundary[0, 1], "pipe", 1)
    returned = shifted(boundary[0, 0], "pipe", -1)
    onehot = (tokens[:, None] == jnp.arange(table.shape[0], dtype=jnp.int32)[None, :]).astype(
        jnp.bfloat16
    )
    embedded = jnp.dot(onehot, table, preferred_element_type=jnp.float32).astype(jnp.bfloat16)
    x = jnp.where(segment_index == 0, embedded, arrived)
    cot = jnp.where(segment_index == segments - 1, loss_grad, returned)
    sav = saved_in[0]
    x32, sav32 = x.astype(jnp.float32), sav.astype(jnp.float32)
    squares = width_sum(jnp.stack([jnp.sum(x32 * x32, axis=1), jnp.sum(sav32 * sav32, axis=1)]))
    scales = lax.rsqrt(squares / D + epsilon)
    length, channels = x.shape
    modes = decay_rate.shape[1]
    steps = length // ROWS
    sf = jnp.broadcast_to(scales[0][:, None], (length, LANES))
    sb = jnp.broadcast_to(scales[1][:, None], (length, LANES))
    chunk = min(CHUNK, channels)
    grid = (channels // chunk,)
    tall = pl.BlockSpec((length, chunk), lambda c: (0, c))
    scale_spec = pl.BlockSpec((length, LANES), lambda c: (0, 0))
    row = pl.BlockSpec((1, chunk), lambda c: (0, c))
    mode_spec = pl.BlockSpec((modes, chunk), lambda c: (0, c))
    e_spec = pl.BlockSpec((3, modes, ROWS, chunk), lambda c: (0, 0, 0, c))
    params = pltpu.CompilerParams(vmem_limit_bytes=40 * 1024 * 1024)
    f32 = jnp.float32
    work = length * channels
    entries, ends = pl.pallas_call(
        states_kernel,
        grid=grid,
        in_specs=[tall, tall, tall, scale_spec, scale_spec, row, mode_spec],
        out_specs=[e_spec, pl.BlockSpec((3, modes, chunk), lambda c: (0, 0, c))],
        out_shape=[
            jax.ShapeDtypeStruct((3, modes, ROWS, channels), f32),
            jax.ShapeDtypeStruct((3, modes, channels), jnp.bfloat16),
        ],
        scratch_shapes=[pltpu.VMEM((3, length, LANES), f32), pltpu.VMEM((modes, LANES), f32)],
        compiler_params=params,
        cost_estimate=pl.CostEstimate(flops=96 * work, bytes_accessed=18 * work, transcendentals=0),
    )(x, sav, cot, sf, sb, gain, decay_rate[0])
    gathered = lax.all_gather(ends, "ctx")
    mine = lax.axis_index("ctx").astype(jnp.int32).reshape(1)
    out, part, gain_grad, skip_grad, inner = pl.pallas_call(
        finish_kernel,
        grid=grid,
        in_specs=[
            pl.BlockSpec(memory_space=pltpu.SMEM), tall, tall, tall, scale_spec, scale_spec,
            row, row, mode_spec, mode_spec, e_spec,
            pl.BlockSpec((gathered.shape[0], 3, modes, chunk), lambda c: (0, 0, 0, c)),
        ],
        out_specs=[tall, tall, row, row, pl.BlockSpec((steps, ROWS, LANES), lambda c: (0, 0, 0))],
        out_shape=[
            jax.ShapeDtypeStruct((length, channels), jnp.bfloat16),
            jax.ShapeDtypeStruct((length, channels), f32),
            jax.ShapeDtypeStruct((1, channels), f32),
            jax.ShapeDtypeStruct((1, channels), f32),
            jax.ShapeDtypeStruct((steps, ROWS, LANES), f32),
        ],
        scratch_shapes=[pltpu.VMEM((3, length, LANES), f32), pltpu.VMEM((3, length, LANES), f32)],
        compiler_params=params,
        cost_estimate=pl.CostEstimate(flops=150 * work, bytes_accessed=24 * work, transcendentals=0),
    )(mine, x, sav, cot, sf, sb, gain, skip, residue[0], decay_rate[0], entries, gathered)
    inner_sum = width_sum(jnp.sum(inner, axis=2)).T.reshape(length)
    factor = (scales[1] ** 2 * inner_sum / D)[:, None]
    input_grad = (part - sav32 * factor).astype(jnp.bfloat16)
    return (out[None], input_grad[None], gain_grad[None], skip_grad[None])


def solution(mesh):
    in_specs = (
        P("ctx"),
        P(None, "width"),
        P("pipe", None, "ctx", "width"),
        P("pipe", "ctx", "width"),
        P("ctx", "width"),
        P("pipe", "width"),
        P("pipe", "width"),
        P("pipe", None, "width"),
        P("pipe", None, "width"),
    )
    out_specs = (
        P("pipe", "ctx", "width"),
        P("pipe", "ctx", "width"),
        P("pipe", "ctx", "width"),
        P("pipe", "ctx", "width"),
    )
    return jax.shard_map(local, mesh=mesh, in_specs=in_specs, out_specs=out_specs, check_vma=False)
```

```python
import jax
import jax.numpy as jnp
from jax import lax
from jax.experimental import pallas as pl
from jax.experimental.pallas import tpu as pltpu
from jax.sharding import PartitionSpec as P

D = 8192
ROWS = 8
LANES = 128
CHUNK = 512
VMEM = 58 * 1024 * 1024
epsilon = 1e-06


def shifted(value, axis, steps):
    count = lax.axis_size(axis)
    initial, last = (max(0, -steps), min(count, count - steps))
    return lax.ppermute(value, axis, [(source, source + steps) for source in range(initial, last)])


def width_sum(value):
    if lax.axis_size("width") == 2:
        return value + lax.ppermute(value, "width", [(0, 1), (1, 0)])
    return lax.psum(value, "width")


def wide(row):
    return jnp.broadcast_to(row, (ROWS, LANES))


def states_kernel(x_ref, sav_ref, cot_ref, sf_ref, sb_ref, gain_ref, decay_ref,
                  e_ref, recv_ref, sig, last, end_ref, send_sem, recv_sem):
    peers = recv_ref.shape[0] + 1
    mine = lax.axis_index("ctx")
    chunk = x_ref.shape[1]
    chunks = end_ref.shape[2] // chunk
    step = pl.program_id(0)

    def copy(c, far, rev):
        lanes = pl.ds(pl.multiple_of(c * chunk, chunk), chunk)
        parts = pl.ds(2, 1) if rev else pl.ds(0, 2)
        index = 2 * (far - 1) + rev
        return pltpu.make_async_remote_copy(
            src_ref=end_ref.at[parts, :, lanes],
            dst_ref=recv_ref.at[far - 1, parts, :, lanes],
            send_sem=send_sem.at[c, index],
            recv_sem=recv_sem.at[c, index],
            device_id={"ctx": jnp.maximum(mine - far, 0) if rev else jnp.minimum(mine + far, peers - 1)},
            device_id_type=pl.DeviceIdType.MESH,
        )

    @pl.when(step == 0)
    def _():
        barrier = pltpu.get_barrier_semaphore()
        for far in range(1, peers):
            pl.semaphore_signal(barrier, inc=1, device_id={"ctx": lax.rem(mine + far, peers)},
                                device_id_type=pl.DeviceIdType.MESH)
        pl.semaphore_wait(barrier, peers - 1)

    length = x_ref.shape[0]
    steps = length // ROWS
    modes = decay_ref.shape[0]
    place = lax.broadcasted_iota(jnp.int32, (ROWS, LANES), 0)

    def group(g, carry):
        lanes = pl.ds(pl.multiple_of(g * LANES, LANES), LANES)
        gain = gain_ref[:, lanes]
        back = sav_ref[:, lanes].astype(jnp.float32) * sb_ref[...] * gain
        sig[0] = x_ref[:, lanes].astype(jnp.float32) * sf_ref[...] * gain
        sig[1] = back
        sig[2] = cot_ref[:, lanes].astype(jnp.float32) * back
        damping = decay_ref[:, lanes]
        a_all = jnp.exp(-damping)
        stride_all = jnp.exp(-damping * float(steps))
        a = [wide(a_all[k:k + 1]) for k in range(modes)]
        for q in range(3):
            rev = q == 2
            order = range(steps - 1, -1, -1) if rev else range(steps)
            state = None
            for j in order:
                piece = sig[q, pl.ds(j, ROWS, stride=steps), :]
                if state is None:
                    state = [piece] * modes
                else:
                    state = [a[k] * state[k] + piece for k in range(modes)]
            for k in range(modes):
                power = wide(stride_all[k:k + 1])
                total = state[k]
                hop = 1
                while hop < ROWS:
                    near = (place < ROWS - hop) if rev else (place >= hop)
                    moved = pltpu.roll(total, ROWS - hop if rev else hop, 0)
                    total = total + jnp.where(near, power * moved, 0.0)
                    power = power * power
                    hop *= 2
                near = (place < ROWS - 1) if rev else (place >= 1)
                moved = pltpu.roll(total, ROWS - 1 if rev else 1, 0)
                e_ref[q, k, :, lanes] = jnp.where(near, moved, 0.0)
                edge = 0 if rev else ROWS - 1
                last[k:k + 1, :] = total[edge:edge + 1, :]
            here = pl.ds(pl.multiple_of(step * chunk + g * LANES, LANES), LANES)
            end_ref[q, :, here] = last[...].astype(end_ref.dtype)
        return carry

    lax.fori_loop(0, chunk // LANES, group, 0)

    for far in range(1, peers):
        @pl.when(mine + far < peers)
        def _():
            copy(step, far, 0).start()

        @pl.when(mine >= far)
        def _():
            copy(step, far, 1).start()

    @pl.when(step == chunks - 1)
    def _():
        def finish(c, carry):
            for far in range(1, peers):
                @pl.when(mine + far < peers)
                def _():
                    copy(c, far, 0).wait_send()
                    copy(c, far, 1).wait_recv()

                @pl.when(mine >= far)
                def _():
                    copy(c, far, 1).wait_send()
                    copy(c, far, 0).wait_recv()
            return carry

        lax.fori_loop(0, chunks, finish, 0)


def finish_kernel(mine_ref, x_ref, sav_ref, cot_ref, sf_ref, sb_ref, gain_ref, skip_ref,
                  residue_ref, decay_ref, e_ref, ends_ref,
                  out_ref, part_ref, gg_ref, sg_ref, acc_ref, sig, res):
    length = x_ref.shape[0]
    steps = length // ROWS
    modes = decay_ref.shape[0]
    peers = ends_ref.shape[0] + 1
    mine = mine_ref[0]
    place = lax.broadcasted_iota(jnp.int32, (ROWS, LANES), 0).astype(jnp.float32)

    @pl.when(pl.program_id(0) == 0)
    def _():
        acc_ref[...] = jnp.zeros_like(acc_ref)

    def group(g, carry):
        lanes = pl.ds(pl.multiple_of(g * LANES, LANES), LANES)
        gain = gain_ref[:, lanes]
        gain_w = wide(gain)
        sig[0] = x_ref[:, lanes].astype(jnp.float32)
        sig[1] = sav_ref[:, lanes].astype(jnp.float32) * sb_ref[...]
        sig[2] = cot_ref[:, lanes].astype(jnp.float32)
        damping = decay_ref[:, lanes]
        a_all = jnp.exp(-damping)
        coefs = residue_ref[:, lanes] * jnp.sqrt(1.0 - jnp.exp(-2.0 * damping))
        whole = jnp.exp(-damping * float(length))
        entering = []
        for q in range(3):
            total = jnp.zeros((modes, LANES), jnp.float32)
            for far in range(peers - 1, 0, -1):
                reached = (mine + far < peers) if q == 2 else (mine >= far)
                longer = whole * total + ends_ref[far - 1, q, :, lanes].astype(jnp.float32)
                total = jnp.where(reached, longer, total)
            entering.append(total)
        kernel = []
        power = coefs
        for n in range(steps):
            kernel.append(wide(jnp.sum(power, axis=0, keepdims=True)))
            power = power * a_all
        kernel[0] = kernel[0] + wide(skip_ref[:, lanes])

        def rows(i):
            return pl.ds(i, ROWS, stride=steps)

        def conv(q, pieces, emit):
            rev = q == 2
            ago = (float(ROWS - 1) - place) if rev else place
            decayed = []
            for k in range(modes):
                gap = jnp.exp(wide(damping[k:k + 1]) * (ago * float(-steps)))
                state = e_ref[q, k, :, lanes] + gap * wide(entering[q][k:k + 1])
                decayed.append(wide(coefs[k:k + 1]) * state)
            a = [wide(a_all[k:k + 1]) for k in range(modes)]
            for n in range(steps):
                decayed = [a[k] * decayed[k] for k in range(modes)]
                terms = decayed + [kernel[n - m] * pieces[steps - 1 - m if rev else m]
                                   for m in range(n + 1)]
                sums = terms[:4]
                for index, term in enumerate(terms[4:]):
                    sums[index % 4] = sums[index % 4] + term
                emit(steps - 1 - n if rev else n, (sums[0] + sums[1]) + (sums[2] + sums[3]))

        raw = [sig[0, rows(i), :] for i in range(steps)]
        normed = [raw[i] * sf_ref[rows(i), :] * gain_w for i in range(steps)]

        def emit_out(i, value):
            res[0, rows(i), :] = sig[0, rows(i), :] + sig[0, rows(i), :] * sf_ref[rows(i), :] * gain_w * value

        conv(0, normed, emit_out)
        out_ref[:, lanes] = res[0].astype(out_ref.dtype)

        back = [sig[1, rows(i), :] * gain_w for i in range(steps)]

        def emit_mixed(i, value):
            res[1, rows(i), :] = sig[2, rows(i), :] * value

        conv(1, back, emit_mixed)

        mix = [sig[2, rows(i), :] * back[i] for i in range(steps)]
        skip_sum = mix[0] * back[0]
        for i in range(1, steps):
            skip_sum = skip_sum + mix[i] * back[i]
        sg_ref[:, lanes] = jnp.sum(skip_sum, axis=0, keepdims=True)
        gain_sums = [jnp.zeros((ROWS, LANES), jnp.float32)]

        def emit_grad(i, value):
            norm = res[1, rows(i), :] + value
            unit = sig[1, rows(i), :]
            gain_sums[0] = gain_sums[0] + norm * unit
            scaled = gain_w * norm
            acc_ref[i] = acc_ref[i] + scaled * unit
            res[2, rows(i), :] = sig[2, rows(i), :] + sb_ref[rows(i), :] * scaled

        conv(2, mix, emit_grad)
        part_ref[:, lanes] = res[2]
        gg_ref[:, lanes] = jnp.sum(gain_sums[0], axis=0, keepdims=True)
        return carry

    lax.fori_loop(0, x_ref.shape[1] // LANES, group, 0)


def local(tokens, table, boundary, saved_in, loss_grad, gain, skip, residue, decay_rate):
    segment_index = lax.axis_index("pipe")
    segments = lax.axis_size("pipe")
    arrived = shifted(boundary[0, 1], "pipe", 1)
    returned = shifted(boundary[0, 0], "pipe", -1)
    onehot = (tokens[:, None] == jnp.arange(table.shape[0], dtype=jnp.int32)[None, :]).astype(
        jnp.bfloat16
    )
    embedded = jnp.dot(onehot, table, preferred_element_type=jnp.float32).astype(jnp.bfloat16)
    sav = saved_in[0]

    def squares_of(value):
        value = value.astype(jnp.float32)
        return jnp.sum(value * value, axis=1)

    squares = width_sum(
        jnp.stack([squares_of(boundary[0, 1]), squares_of(sav), squares_of(embedded)])
    )
    square_fwd = jnp.where(segment_index == 0, squares[2], shifted(squares[0], "pipe", 1))
    x = jnp.where(segment_index == 0, embedded, arrived)
    cot = jnp.where(segment_index == segments - 1, loss_grad, returned)
    scales = lax.rsqrt(jnp.stack([square_fwd, squares[1]]) / D + epsilon)
    length, channels = x.shape
    modes = decay_rate.shape[1]
    steps = length // ROWS
    sf = jnp.broadcast_to(scales[0][:, None], (length, LANES))
    sb = jnp.broadcast_to(scales[1][:, None], (length, LANES))
    chunk = min(CHUNK, channels)
    grid = (channels // chunk,)
    tall = pl.BlockSpec((length, chunk), lambda c: (0, c))
    scale_spec = pl.BlockSpec((length, LANES), lambda c: (0, 0))
    row = pl.BlockSpec((1, chunk), lambda c: (0, c))
    mode_spec = pl.BlockSpec((modes, chunk), lambda c: (0, c))
    e_spec = pl.BlockSpec((3, modes, ROWS, chunk), lambda c: (0, 0, 0, c))
    params = pltpu.CompilerParams(vmem_limit_bytes=VMEM)
    f32 = jnp.float32
    work = length * channels
    peers = lax.axis_size("ctx")
    copies = (channels // chunk, 2 * (peers - 1))
    entries, received = pl.pallas_call(
        states_kernel,
        grid=grid,
        in_specs=[tall, tall, tall, scale_spec, scale_spec, row, mode_spec],
        out_specs=[e_spec, pl.BlockSpec(memory_space=pl.ANY)],
        out_shape=[
            jax.ShapeDtypeStruct((3, modes, ROWS, channels), f32),
            jax.ShapeDtypeStruct((peers - 1, 3, modes, channels), jnp.bfloat16),
        ],
        scratch_shapes=[
            pltpu.VMEM((3, length, LANES), f32),
            pltpu.VMEM((modes, LANES), f32),
            pltpu.VMEM((3, modes, channels), jnp.bfloat16),
            pltpu.SemaphoreType.DMA(copies),
            pltpu.SemaphoreType.DMA(copies),
        ],
        compiler_params=pltpu.CompilerParams(
            vmem_limit_bytes=VMEM, collective_id=0, has_side_effects=True
        ),
        cost_estimate=pl.CostEstimate(flops=96 * work, bytes_accessed=18 * work, transcendentals=0),
    )(x, sav, cot, sf, sb, gain, decay_rate[0])
    mine = lax.axis_index("ctx").astype(jnp.int32).reshape(1)
    out, part, gain_grad, skip_grad, inner = pl.pallas_call(
        finish_kernel,
        grid=grid,
        in_specs=[
            pl.BlockSpec(memory_space=pltpu.SMEM), tall, tall, tall, scale_spec, scale_spec,
            row, row, mode_spec, mode_spec, e_spec,
            pl.BlockSpec((peers - 1, 3, modes, chunk), lambda c: (0, 0, 0, c)),
        ],
        out_specs=[tall, tall, row, row, pl.BlockSpec((steps, ROWS, LANES), lambda c: (0, 0, 0))],
        out_shape=[
            jax.ShapeDtypeStruct((length, channels), jnp.bfloat16),
            jax.ShapeDtypeStruct((length, channels), f32),
            jax.ShapeDtypeStruct((1, channels), f32),
            jax.ShapeDtypeStruct((1, channels), f32),
            jax.ShapeDtypeStruct((steps, ROWS, LANES), f32),
        ],
        scratch_shapes=[pltpu.VMEM((3, length, LANES), f32), pltpu.VMEM((3, length, LANES), f32)],
        compiler_params=params,
        cost_estimate=pl.CostEstimate(flops=150 * work, bytes_accessed=24 * work, transcendentals=0),
    )(mine, x, sav, cot, sf, sb, gain, skip, residue[0], decay_rate[0], entries, received)
    inner_sum = width_sum(jnp.sum(inner, axis=2)).T.reshape(length)
    factor = (scales[1] ** 2 * inner_sum / D)[:, None]
    input_grad = (part - sav.astype(f32) * factor).astype(jnp.bfloat16)
    return (out[None], input_grad[None], gain_grad[None], skip_grad[None])


def solution(mesh):
    in_specs = (
        P("ctx"),
        P(None, "width"),
        P("pipe", None, "ctx", "width"),
        P("pipe", "ctx", "width"),
        P("ctx", "width"),
        P("pipe", "width"),
        P("pipe", "width"),
        P("pipe", None, "width"),
        P("pipe", None, "width"),
    )
    out_specs = (
        P("pipe", "ctx", "width"),
        P("pipe", "ctx", "width"),
        P("pipe", "ctx", "width"),
        P("pipe", "ctx", "width"),
    )
    return jax.shard_map(local, mesh=mesh, in_specs=in_specs, out_specs=out_specs, check_vma=False)
```

```python
import functools

import jax
import jax.numpy as jnp
from jax import lax
from jax.experimental import pallas as pl
from jax.experimental.pallas import tpu as pltpu
from jax.sharding import PartitionSpec as P

D = 8192
ROWS = 8
LANES = 128
CHUNK = 512
VMEM = 58 * 1024 * 1024
epsilon = 1e-06


def shifted(value, axis, steps):
    count = lax.axis_size(axis)
    initial, last = (max(0, -steps), min(count, count - steps))
    return lax.ppermute(value, axis, [(source, source + steps) for source in range(initial, last)])


def width_sum(value):
    if lax.axis_size("width") == 2:
        return value + lax.ppermute(value, "width", [(0, 1), (1, 0)])
    return lax.psum(value, "width")


def wide(row):
    return jnp.broadcast_to(row, (ROWS, LANES))


def step_kernel(segments, emb_ref, arr_ref, sav_ref, loss_ref, ret_ref, scale_ref, gain_ref,
                decay_ref, skip_ref, residue_ref,
                out_ref, part_ref, gg_ref, sg_ref, acc_ref,
                sig, res, last, e_all, end_ref, recv_ref, send_sem, recv_sem):
    peers = recv_ref.shape[0] + 1
    mine = lax.axis_index("ctx")
    segment = lax.axis_index("pipe")
    chunk = sav_ref.shape[1]
    chunks = end_ref.shape[2] // chunk
    step = pl.program_id(0)
    sf_ref, sb_ref = scale_ref.at[0], scale_ref.at[1]
    length = sav_ref.shape[0]
    steps = length // ROWS
    modes = decay_ref.shape[0]

    def incoming(lanes):
        return jnp.where(segment == 0, emb_ref[:, lanes].astype(jnp.float32),
                         arr_ref[:, lanes].astype(jnp.float32))

    def cotangent(lanes):
        return jnp.where(segment == segments - 1, loss_ref[:, lanes].astype(jnp.float32),
                         ret_ref[:, lanes].astype(jnp.float32))

    def copy(c, far, rev):
        lanes = pl.ds(pl.multiple_of(c * chunk, chunk), chunk)
        parts = pl.ds(2, 1) if rev else pl.ds(0, 2)
        index = 2 * (far - 1) + rev
        return pltpu.make_async_remote_copy(
            src_ref=end_ref.at[parts, :, lanes],
            dst_ref=recv_ref.at[far - 1, parts, :, lanes],
            send_sem=send_sem.at[c, index],
            recv_sem=recv_sem.at[c, index],
            device_id={"ctx": jnp.maximum(mine - far, 0) if rev else jnp.minimum(mine + far, peers - 1)},
            device_id_type=pl.DeviceIdType.MESH,
        )

    @pl.when(step == 0)
    def _():
        barrier = pltpu.get_barrier_semaphore()
        for far in range(1, peers):
            pl.semaphore_signal(barrier, inc=1, device_id={"ctx": lax.rem(mine + far, peers)},
                                device_id_type=pl.DeviceIdType.MESH)
        pl.semaphore_wait(barrier, peers - 1)
        acc_ref[...] = jnp.zeros_like(acc_ref)

    @pl.when(step < chunks)
    def _():
        place = lax.broadcasted_iota(jnp.int32, (ROWS, LANES), 0)

        def group(g, carry):
            lanes = pl.ds(pl.multiple_of(g * LANES, LANES), LANES)
            gain = gain_ref[:, lanes]
            back = sav_ref[:, lanes].astype(jnp.float32) * sb_ref[...] * gain
            sig[0] = incoming(lanes) * sf_ref[...] * gain
            sig[1] = back
            sig[2] = cotangent(lanes) * back
            damping = decay_ref[:, lanes]
            here = pl.ds(pl.multiple_of(step * chunk + g * LANES, LANES), LANES)
            a_all = jnp.exp(-damping)
            stride_all = jnp.exp(-damping * float(steps))
            a = [wide(a_all[k:k + 1]) for k in range(modes)]
            for q in range(3):
                rev = q == 2
                order = range(steps - 1, -1, -1) if rev else range(steps)
                state = None
                for j in order:
                    piece = sig[q, pl.ds(j, ROWS, stride=steps), :]
                    if state is None:
                        state = [piece] * modes
                    else:
                        state = [a[k] * state[k] + piece for k in range(modes)]
                for k in range(modes):
                    power = wide(stride_all[k:k + 1])
                    total = state[k]
                    hop = 1
                    while hop < ROWS:
                        near = (place < ROWS - hop) if rev else (place >= hop)
                        moved = pltpu.roll(total, ROWS - hop if rev else hop, 0)
                        total = total + jnp.where(near, power * moved, 0.0)
                        power = power * power
                        hop *= 2
                    near = (place < ROWS - 1) if rev else (place >= 1)
                    moved = pltpu.roll(total, ROWS - 1 if rev else 1, 0)
                    e_all[q, k, :, here] = jnp.where(near, moved, 0.0)
                    edge = 0 if rev else ROWS - 1
                    last[k:k + 1, :] = total[edge:edge + 1, :]
                end_ref[q, :, here] = last[...].astype(end_ref.dtype)
            return carry

        lax.fori_loop(0, chunk // LANES, group, 0)

        for far in range(1, peers):
            @pl.when(mine + far < peers)
            def _():
                copy(step, far, 0).start()

            @pl.when(mine >= far)
            def _():
                copy(step, far, 1).start()

    @pl.when(step >= chunks)
    def _():
        place = lax.broadcasted_iota(jnp.int32, (ROWS, LANES), 0).astype(jnp.float32)

        c = step - chunks
        for far in range(1, peers):
            @pl.when(mine + far < peers)
            def _():
                copy(c, far, 0).wait_send()
                copy(c, far, 1).wait_recv()

            @pl.when(mine >= far)
            def _():
                copy(c, far, 1).wait_send()
                copy(c, far, 0).wait_recv()

        def group(g, carry):
            lanes = pl.ds(pl.multiple_of(g * LANES, LANES), LANES)
            gain = gain_ref[:, lanes]
            gain_w = wide(gain)
            sig[0] = incoming(lanes)
            sig[1] = sav_ref[:, lanes].astype(jnp.float32) * sb_ref[...]
            sig[2] = cotangent(lanes)
            damping = decay_ref[:, lanes]
            a_all = jnp.exp(-damping)
            coefs = residue_ref[:, lanes] * jnp.sqrt(1.0 - jnp.exp(-2.0 * damping))
            here = pl.ds(pl.multiple_of(c * chunk + g * LANES, LANES), LANES)
            whole = jnp.exp(-damping * float(length))
            entering = []
            for q in range(3):
                total = jnp.zeros((modes, LANES), jnp.float32)
                for far in range(peers - 1, 0, -1):
                    reached = (mine + far < peers) if q == 2 else (mine >= far)
                    longer = whole * total + recv_ref[far - 1, q, :, here].astype(jnp.float32)
                    total = jnp.where(reached, longer, total)
                entering.append(total)
            kernel = []
            power = coefs
            for n in range(steps):
                kernel.append(wide(jnp.sum(power, axis=0, keepdims=True)))
                power = power * a_all
            kernel[0] = kernel[0] + wide(skip_ref[:, lanes])

            def rows(i):
                return pl.ds(i, ROWS, stride=steps)

            def conv(q, pieces, emit):
                rev = q == 2
                ago = (float(ROWS - 1) - place) if rev else place
                decayed = []
                for k in range(modes):
                    gap = jnp.exp(wide(damping[k:k + 1]) * (ago * float(-steps)))
                    state = e_all[q, k, :, here] + gap * wide(entering[q][k:k + 1])
                    decayed.append(wide(coefs[k:k + 1]) * state)
                a = [wide(a_all[k:k + 1]) for k in range(modes)]
                for n in range(steps):
                    decayed = [a[k] * decayed[k] for k in range(modes)]
                    terms = decayed + [kernel[n - m] * pieces[steps - 1 - m if rev else m]
                                       for m in range(n + 1)]
                    sums = terms[:4]
                    for index, term in enumerate(terms[4:]):
                        sums[index % 4] = sums[index % 4] + term
                    emit(steps - 1 - n if rev else n, (sums[0] + sums[1]) + (sums[2] + sums[3]))

            raw = [sig[0, rows(i), :] for i in range(steps)]
            normed = [raw[i] * sf_ref[rows(i), :] * gain_w for i in range(steps)]

            def emit_out(i, value):
                res[0, rows(i), :] = sig[0, rows(i), :] + sig[0, rows(i), :] * sf_ref[rows(i), :] * gain_w * value

            conv(0, normed, emit_out)
            out_ref[:, lanes] = res[0].astype(out_ref.dtype)

            back = [sig[1, rows(i), :] * gain_w for i in range(steps)]

            def emit_mixed(i, value):
                res[1, rows(i), :] = sig[2, rows(i), :] * value

            conv(1, back, emit_mixed)

            mix = [sig[2, rows(i), :] * back[i] for i in range(steps)]
            skip_sum = mix[0] * back[0]
            for i in range(1, steps):
                skip_sum = skip_sum + mix[i] * back[i]
            sg_ref[:, lanes] = jnp.sum(skip_sum, axis=0, keepdims=True)
            gain_sums = [jnp.zeros((ROWS, LANES), jnp.float32)]

            def emit_grad(i, value):
                norm = res[1, rows(i), :] + value
                unit = sig[1, rows(i), :]
                gain_sums[0] = gain_sums[0] + norm * unit
                scaled = gain_w * norm
                acc_ref[i] = acc_ref[i] + scaled * unit
                res[2, rows(i), :] = sig[2, rows(i), :] + sb_ref[rows(i), :] * scaled

            conv(2, mix, emit_grad)
            part_ref[:, lanes] = res[2]
            gg_ref[:, lanes] = jnp.sum(gain_sums[0], axis=0, keepdims=True)
            return carry

        lax.fori_loop(0, chunk // LANES, group, 0)


def local(tokens, table, boundary, saved_in, loss_grad, gain, skip, residue, decay_rate):
    segment_index = lax.axis_index("pipe")
    segments = lax.axis_size("pipe")
    arrived = shifted(boundary[0, 1], "pipe", 1)
    returned = shifted(boundary[0, 0], "pipe", -1)
    onehot = (tokens[:, None] == jnp.arange(table.shape[0], dtype=jnp.int32)[None, :]).astype(
        jnp.bfloat16
    )
    embedded = jnp.dot(onehot, table, preferred_element_type=jnp.float32).astype(jnp.bfloat16)
    sav = saved_in[0]

    def squares_of(value):
        value = value.astype(jnp.float32)
        return jnp.sum(value * value, axis=1)

    squares = width_sum(
        jnp.stack([squares_of(boundary[0, 1]), squares_of(sav), squares_of(embedded)])
    )
    square_fwd = jnp.where(segment_index == 0, squares[2], shifted(squares[0], "pipe", 1))
    scales = lax.rsqrt(jnp.stack([square_fwd, squares[1]]) / D + epsilon)
    length, channels = sav.shape
    modes = decay_rate.shape[1]
    steps = length // ROWS
    scale_tiles = jnp.broadcast_to(scales[:, :, None], (2, length, LANES))
    chunk = min(CHUNK, channels)
    chunks = channels // chunk
    peers = lax.axis_size("ctx")
    f32 = jnp.float32
    work = length * channels

    def both(height):
        return pl.BlockSpec((height, chunk), lambda s: (0, lax.rem(s, chunks)))

    def late(height):
        return pl.BlockSpec((height, chunk), lambda s: (0, jnp.maximum(s - chunks, 0)))

    out, part, gain_grad, skip_grad, inner = pl.pallas_call(
        functools.partial(step_kernel, segments),
        grid=(2 * chunks,),
        in_specs=[
            both(length), both(length), both(length), both(length), both(length),
            pl.BlockSpec((2, length, LANES), lambda s: (0, 0, 0)),
            both(1), both(modes), late(1), late(modes),
        ],
        out_specs=[late(length), late(length), late(1), late(1),
                   pl.BlockSpec((steps, ROWS, LANES), lambda s: (0, 0, 0))],
        out_shape=[
            jax.ShapeDtypeStruct((length, channels), jnp.bfloat16),
            jax.ShapeDtypeStruct((length, channels), f32),
            jax.ShapeDtypeStruct((1, channels), f32),
            jax.ShapeDtypeStruct((1, channels), f32),
            jax.ShapeDtypeStruct((steps, ROWS, LANES), f32),
        ],
        scratch_shapes=[
            pltpu.VMEM((3, length, LANES), f32),
            pltpu.VMEM((3, length, LANES), f32),
            pltpu.VMEM((modes, LANES), f32),
            pltpu.VMEM((3, modes, ROWS, channels), f32),
            pltpu.VMEM((3, modes, channels), jnp.bfloat16),
            pltpu.VMEM((peers - 1, 3, modes, channels), jnp.bfloat16),
            pltpu.SemaphoreType.DMA((chunks, 2 * (peers - 1))),
            pltpu.SemaphoreType.DMA((chunks, 2 * (peers - 1))),
        ],
        compiler_params=pltpu.CompilerParams(
            vmem_limit_bytes=VMEM, collective_id=0, has_side_effects=True
        ),
        cost_estimate=pl.CostEstimate(flops=246 * work, bytes_accessed=26 * work, transcendentals=0),
    )(embedded, arrived, sav, loss_grad, returned, scale_tiles, gain, decay_rate[0], skip, residue[0])
    inner_sum = width_sum(jnp.sum(inner, axis=2)).T.reshape(length)
    factor = (scales[1] ** 2 * inner_sum / D)[:, None]
    input_grad = (part - sav.astype(f32) * factor).astype(jnp.bfloat16)
    return (out[None], input_grad[None], gain_grad[None], skip_grad[None])


def solution(mesh):
    in_specs = (
        P("ctx"),
        P(None, "width"),
        P("pipe", None, "ctx", "width"),
        P("pipe", "ctx", "width"),
        P("ctx", "width"),
        P("pipe", "width"),
        P("pipe", "width"),
        P("pipe", None, "width"),
        P("pipe", None, "width"),
    )
    out_specs = (
        P("pipe", "ctx", "width"),
        P("pipe", "ctx", "width"),
        P("pipe", "ctx", "width"),
        P("pipe", "ctx", "width"),
    )
    return jax.shard_map(local, mesh=mesh, in_specs=in_specs, out_specs=out_specs, check_vma=False)
```

```python
import functools

import jax
import jax.numpy as jnp
from jax import lax
from jax.experimental import pallas as pl
from jax.experimental.pallas import tpu as pltpu
from jax.sharding import PartitionSpec as P

D = 8192
ROWS = 8
LANES = 128
CHUNK = 512
VMEM = 58 * 1024 * 1024
epsilon = 1e-06


def width_sum(value):
    if lax.axis_size("width") == 2:
        return value + lax.ppermute(value, "width", [(0, 1), (1, 0)])
    return lax.psum(value, "width")


def wide(row):
    return jnp.broadcast_to(row, (ROWS, LANES))


def summed(terms):
    sums = terms[:4]
    for index, term in enumerate(terms[4:]):
        sums[index % 4] = sums[index % 4] + term
    total = sums[0]
    for term in sums[1:]:
        total = total + term
    return total


def step_kernel(segments, bound_ref, emb_ref, sav_ref, loss_ref, square_ref, gain_ref,
                decay_ref, skip_ref, residue_ref,
                out_ref, part_ref, gg_ref, sg_ref, acc_ref,
                sig, res, last, e_all, end_ref, recv_ref, rows_ref, scale_ref, came_ref,
                send_sem, recv_sem, row_send, row_recv, tile_sem):
    peers = recv_ref.shape[0] + 1
    mine = lax.axis_index("ctx")
    segment = lax.axis_index("pipe")
    chunk = sav_ref.shape[1]
    chunks = end_ref.shape[2] // chunk
    step = pl.program_id(0)
    sf_ref, sb_ref = scale_ref.at[0], scale_ref.at[1]
    length = sav_ref.shape[0]
    steps = length // ROWS
    modes = decay_ref.shape[0]

    def incoming(here):
        return rows_ref[1, :, here].astype(jnp.float32)

    def cotangent(here):
        return rows_ref[0, :, here].astype(jnp.float32)

    def move(c, forward):
        lanes = pl.ds(pl.multiple_of(c * chunk, chunk), chunk)
        target = jnp.minimum(segment + 1, segments - 1) if forward else jnp.maximum(segment - 1, 0)
        return pltpu.make_async_remote_copy(
            src_ref=bound_ref.at[0, forward, :, lanes],
            dst_ref=rows_ref.at[forward, :, lanes],
            send_sem=row_send.at[c, forward],
            recv_sem=row_recv.at[c, forward],
            device_id={"pipe": target},
            device_id_type=pl.DeviceIdType.MESH,
        )

    def move_tile():
        return pltpu.make_async_remote_copy(
            src_ref=square_ref.at[0],
            dst_ref=came_ref,
            send_sem=tile_sem.at[0],
            recv_sem=tile_sem.at[1],
            device_id={"pipe": jnp.minimum(segment + 1, segments - 1)},
            device_id_type=pl.DeviceIdType.MESH,
        )

    first = segment == 0
    final = segment == segments - 1

    def copy(c, far, rev):
        lanes = pl.ds(pl.multiple_of(c * chunk, chunk), chunk)
        parts = pl.ds(2, 1) if rev else pl.ds(0, 2)
        index = 2 * (far - 1) + rev
        return pltpu.make_async_remote_copy(
            src_ref=end_ref.at[parts, :, lanes],
            dst_ref=recv_ref.at[far - 1, parts, :, lanes],
            send_sem=send_sem.at[c, index],
            recv_sem=recv_sem.at[c, index],
            device_id={"ctx": jnp.maximum(mine - far, 0) if rev else jnp.minimum(mine + far, peers - 1)},
            device_id_type=pl.DeviceIdType.MESH,
        )

    @pl.when(step == 0)
    def _():
        barrier = pltpu.get_barrier_semaphore()
        for far in range(1, peers):
            pl.semaphore_signal(barrier, inc=1, device_id={"ctx": lax.rem(mine + far, peers)},
                                device_id_type=pl.DeviceIdType.MESH)

        @pl.when(jnp.logical_not(first))
        def _():
            pl.semaphore_signal(barrier, inc=1, device_id={"pipe": jnp.maximum(segment - 1, 0)},
                                device_id_type=pl.DeviceIdType.MESH)

        @pl.when(jnp.logical_not(final))
        def _():
            pl.semaphore_signal(barrier, inc=1,
                                device_id={"pipe": jnp.minimum(segment + 1, segments - 1)},
                                device_id_type=pl.DeviceIdType.MESH)

        around = jnp.where(first, 0, 1) + jnp.where(final, 0, 1)
        pl.semaphore_wait(barrier, peers - 1 + around)

        @pl.when(jnp.logical_not(final))
        def _():
            move_tile().start()

        for c in range(chunks):
            @pl.when(jnp.logical_not(final))
            def _():
                move(c, 1).start()

            @pl.when(jnp.logical_not(first))
            def _():
                move(c, 0).start()

        acc_ref[...] = jnp.zeros_like(acc_ref)
        scale_ref[1] = lax.rsqrt(square_ref[1] / D + epsilon)

        @pl.when(first)
        def _():
            scale_ref[0] = lax.rsqrt(square_ref[2] / D + epsilon)

        @pl.when(jnp.logical_not(first))
        def _():
            move_tile().wait_recv()
            scale_ref[0] = lax.rsqrt(came_ref[...] / D + epsilon)

        @pl.when(jnp.logical_not(final))
        def _():
            move_tile().wait_send()

    @pl.when(step < chunks)
    def _():
        block = pl.ds(pl.multiple_of(step * chunk, chunk), chunk)

        @pl.when(first)
        def _():
            rows_ref[1, :, block] = emb_ref[...]

        @pl.when(jnp.logical_not(first))
        def _():
            move(step, 1).wait_recv()

        @pl.when(final)
        def _():
            rows_ref[0, :, block] = loss_ref[...]

        @pl.when(jnp.logical_not(final))
        def _():
            move(step, 0).wait_recv()

        place = lax.broadcasted_iota(jnp.int32, (ROWS, LANES), 0)

        def group(g, carry):
            lanes = pl.ds(pl.multiple_of(g * LANES, LANES), LANES)
            here = pl.ds(pl.multiple_of(step * chunk + g * LANES, LANES), LANES)
            gain = gain_ref[:, lanes]
            back = sav_ref[:, lanes].astype(jnp.float32) * sb_ref[...] * gain
            sig[0] = incoming(here) * sf_ref[...] * gain
            sig[1] = back
            sig[2] = cotangent(here) * back
            damping = decay_ref[:, lanes]
            a_all = jnp.exp(-damping)
            stride_all = jnp.exp(-damping * float(steps))
            a = [wide(a_all[k:k + 1]) for k in range(modes)]
            for q in range(3):
                rev = q == 2
                order = range(steps - 1, -1, -1) if rev else range(steps)
                state = None
                for j in order:
                    piece = sig[q, pl.ds(j, ROWS, stride=steps), :]
                    if state is None:
                        state = [piece] * modes
                    else:
                        state = [a[k] * state[k] + piece for k in range(modes)]
                for k in range(modes):
                    power = wide(stride_all[k:k + 1])
                    total = state[k]
                    hop = 1
                    while hop < ROWS:
                        near = (place < ROWS - hop) if rev else (place >= hop)
                        moved = pltpu.roll(total, ROWS - hop if rev else hop, 0)
                        total = total + jnp.where(near, power * moved, 0.0)
                        power = power * power
                        hop *= 2
                    near = (place < ROWS - 1) if rev else (place >= 1)
                    moved = pltpu.roll(total, ROWS - 1 if rev else 1, 0)
                    e_all[q, k, :, here] = jnp.where(near, moved, 0.0)
                    edge = 0 if rev else ROWS - 1
                    last[k:k + 1, :] = total[edge:edge + 1, :]
                end_ref[q, :, here] = last[...].astype(end_ref.dtype)
            return carry

        lax.fori_loop(0, chunk // LANES, group, 0)

        for far in range(1, peers):
            @pl.when(mine + far < peers)
            def _():
                copy(step, far, 0).start()

            @pl.when(mine >= far)
            def _():
                copy(step, far, 1).start()

    @pl.when(step >= chunks)
    def _():
        place = lax.broadcasted_iota(jnp.int32, (ROWS, LANES), 0).astype(jnp.float32)

        c = step - chunks

        @pl.when(jnp.logical_not(final))
        def _():
            move(c, 1).wait_send()

        @pl.when(jnp.logical_not(first))
        def _():
            move(c, 0).wait_send()

        for far in range(1, peers):
            @pl.when(mine + far < peers)
            def _():
                copy(c, far, 0).wait_send()
                copy(c, far, 1).wait_recv()

            @pl.when(mine >= far)
            def _():
                copy(c, far, 1).wait_send()
                copy(c, far, 0).wait_recv()

        def group(g, carry):
            lanes = pl.ds(pl.multiple_of(g * LANES, LANES), LANES)
            here = pl.ds(pl.multiple_of(c * chunk + g * LANES, LANES), LANES)
            gain = gain_ref[:, lanes]
            gain_w = wide(gain)
            sig[0] = incoming(here)
            sig[1] = sav_ref[:, lanes].astype(jnp.float32) * sb_ref[...]
            sig[2] = cotangent(here)
            damping = decay_ref[:, lanes]
            a_all = jnp.exp(-damping)
            coefs = residue_ref[:, lanes] * jnp.sqrt(1.0 - jnp.exp(-2.0 * damping))
            whole = jnp.exp(-damping * float(length))
            entering = []
            for q in range(3):
                total = jnp.zeros((modes, LANES), jnp.float32)
                for far in range(peers - 1, 0, -1):
                    reached = (mine + far < peers) if q == 2 else (mine >= far)
                    longer = whole * total + recv_ref[far - 1, q, :, here].astype(jnp.float32)
                    total = jnp.where(reached, longer, total)
                entering.append(total)
            kernel = []
            power = coefs
            for n in range(steps):
                kernel.append(wide(jnp.sum(power, axis=0, keepdims=True)))
                power = power * a_all
            kernel[0] = kernel[0] + wide(skip_ref[:, lanes])

            def rows(i):
                return pl.ds(i, ROWS, stride=steps)

            def conv(q, pieces, emit):
                rev = q == 2
                near = []
                for n in range(steps):
                    near.append(summed([kernel[n - m] * pieces[steps - 1 - m if rev else m]
                                        for m in range(n + 1)]))
                ago = (float(ROWS - 1) - place) if rev else place
                decayed = []
                for k in range(modes):
                    gap = jnp.exp(wide(damping[k:k + 1]) * (ago * float(-steps)))
                    state = e_all[q, k, :, here] + gap * wide(entering[q][k:k + 1])
                    decayed.append(wide(coefs[k:k + 1]) * state)
                a = [wide(a_all[k:k + 1]) for k in range(modes)]
                for n in range(steps):
                    decayed = [a[k] * decayed[k] for k in range(modes)]
                    emit(steps - 1 - n if rev else n, summed([near[n]] + decayed))

            raw = [sig[0, rows(i), :] for i in range(steps)]
            normed = [raw[i] * sf_ref[rows(i), :] * gain_w for i in range(steps)]

            def emit_out(i, value):
                res[0, rows(i), :] = sig[0, rows(i), :] + sig[0, rows(i), :] * sf_ref[rows(i), :] * gain_w * value

            conv(0, normed, emit_out)
            out_ref[:, lanes] = res[0].astype(out_ref.dtype)

            back = [sig[1, rows(i), :] * gain_w for i in range(steps)]

            def emit_mixed(i, value):
                res[1, rows(i), :] = sig[2, rows(i), :] * value

            conv(1, back, emit_mixed)

            mix = [sig[2, rows(i), :] * back[i] for i in range(steps)]
            skip_sum = mix[0] * back[0]
            for i in range(1, steps):
                skip_sum = skip_sum + mix[i] * back[i]
            sg_ref[:, lanes] = jnp.sum(skip_sum, axis=0, keepdims=True)
            gain_sums = [jnp.zeros((ROWS, LANES), jnp.float32)]

            def emit_grad(i, value):
                norm = res[1, rows(i), :] + value
                unit = sig[1, rows(i), :]
                gain_sums[0] = gain_sums[0] + norm * unit
                scaled = gain_w * norm
                acc_ref[i] = acc_ref[i] + scaled * unit
                res[2, rows(i), :] = sig[2, rows(i), :] + sb_ref[rows(i), :] * scaled

            conv(2, mix, emit_grad)
            part_ref[:, lanes] = res[2]
            gg_ref[:, lanes] = jnp.sum(gain_sums[0], axis=0, keepdims=True)
            return carry

        lax.fori_loop(0, chunk // LANES, group, 0)


def local(tokens, table, boundary, saved_in, loss_grad, gain, skip, residue, decay_rate):
    segments = lax.axis_size("pipe")
    onehot = (tokens[:, None] == jnp.arange(table.shape[0], dtype=jnp.int32)[None, :]).astype(
        jnp.bfloat16
    )
    embedded = jnp.dot(onehot, table, preferred_element_type=jnp.float32).astype(jnp.bfloat16)
    sav = saved_in[0]

    def squares_of(value):
        value = value.astype(jnp.float32)
        return jnp.sum(value * value, axis=1)

    squares = width_sum(
        jnp.stack([squares_of(boundary[0, 1]), squares_of(sav), squares_of(embedded)])
    )
    length, channels = sav.shape
    modes = decay_rate.shape[1]
    steps = length // ROWS
    squares_wide = jnp.broadcast_to(squares[:, :, None], (3, length, LANES))
    scale_back = lax.rsqrt(squares[1] / D + epsilon)
    chunk = min(CHUNK, channels)
    chunks = channels // chunk
    peers = lax.axis_size("ctx")
    f32 = jnp.float32
    work = length * channels

    def both(height):
        return pl.BlockSpec((height, chunk), lambda s: (0, lax.rem(s, chunks)))

    def early(height):
        return pl.BlockSpec((height, chunk), lambda s: (0, jnp.minimum(s, chunks - 1)))

    def late(height):
        return pl.BlockSpec((height, chunk), lambda s: (0, jnp.maximum(s - chunks, 0)))

    out, part, gain_grad, skip_grad, inner = pl.pallas_call(
        functools.partial(step_kernel, segments),
        grid=(2 * chunks,),
        in_specs=[
            pl.BlockSpec(memory_space=pl.ANY), early(length), both(length), early(length),
            pl.BlockSpec((3, length, LANES), lambda s: (0, 0, 0)),
            both(1), both(modes), late(1), late(modes),
        ],
        out_specs=[late(length), late(length), late(1), late(1),
                   pl.BlockSpec((steps, ROWS, LANES), lambda s: (0, 0, 0))],
        out_shape=[
            jax.ShapeDtypeStruct((length, channels), jnp.bfloat16),
            jax.ShapeDtypeStruct((length, channels), f32),
            jax.ShapeDtypeStruct((1, channels), f32),
            jax.ShapeDtypeStruct((1, channels), f32),
            jax.ShapeDtypeStruct((steps, ROWS, LANES), f32),
        ],
        scratch_shapes=[
            pltpu.VMEM((3, length, LANES), f32),
            pltpu.VMEM((3, length, LANES), f32),
            pltpu.VMEM((modes, LANES), f32),
            pltpu.VMEM((3, modes, ROWS, channels), f32),
            pltpu.VMEM((3, modes, channels), jnp.bfloat16),
            pltpu.VMEM((peers - 1, 3, modes, channels), jnp.bfloat16),
            pltpu.VMEM((2, length, channels), jnp.bfloat16),
            pltpu.VMEM((2, length, LANES), f32),
            pltpu.VMEM((length, LANES), f32),
            pltpu.SemaphoreType.DMA((chunks, 2 * (peers - 1))),
            pltpu.SemaphoreType.DMA((chunks, 2 * (peers - 1))),
            pltpu.SemaphoreType.DMA((chunks, 2)),
            pltpu.SemaphoreType.DMA((chunks, 2)),
            pltpu.SemaphoreType.DMA((2,)),
        ],
        compiler_params=pltpu.CompilerParams(
            vmem_limit_bytes=VMEM, collective_id=0, has_side_effects=True
        ),
        cost_estimate=pl.CostEstimate(flops=246 * work, bytes_accessed=26 * work, transcendentals=0),
    )(boundary, embedded, sav, loss_grad, squares_wide, gain, decay_rate[0], skip, residue[0])
    inner_sum = width_sum(jnp.sum(inner, axis=2)).T.reshape(length)
    factor = (scale_back ** 2 * inner_sum / D)[:, None]
    input_grad = (part - sav.astype(f32) * factor).astype(jnp.bfloat16)
    return (out[None], input_grad[None], gain_grad[None], skip_grad[None])


def solution(mesh):
    in_specs = (
        P("ctx"),
        P(None, "width"),
        P("pipe", None, "ctx", "width"),
        P("pipe", "ctx", "width"),
        P("ctx", "width"),
        P("pipe", "width"),
        P("pipe", "width"),
        P("pipe", None, "width"),
        P("pipe", None, "width"),
    )
    out_specs = (
        P("pipe", "ctx", "width"),
        P("pipe", "ctx", "width"),
        P("pipe", "ctx", "width"),
        P("pipe", "ctx", "width"),
    )
    return jax.shard_map(local, mesh=mesh, in_specs=in_specs, out_specs=out_specs, check_vma=False)
```

```python
import functools

import jax
import jax.numpy as jnp
from jax import lax
from jax.experimental import pallas as pl
from jax.experimental.pallas import tpu as pltpu
from jax.sharding import PartitionSpec as P

D = 8192
ROWS = 8
LANES = 128
CHUNK = 512
VMEM = 58 * 1024 * 1024
epsilon = 1e-06


def width_sum(value):
    if lax.axis_size("width") == 2:
        return value + lax.ppermute(value, "width", [(0, 1), (1, 0)])
    return lax.psum(value, "width")


def wide(row):
    return jnp.broadcast_to(row, (ROWS, LANES))


def summed(terms):
    sums = terms[:4]
    for index, term in enumerate(terms[4:]):
        sums[index % 4] = sums[index % 4] + term
    total = sums[0]
    for term in sums[1:]:
        total = total + term
    return total


def step_kernel(segments, bound_ref, emb_ref, sav_ref, loss_ref, square_ref, gain_ref,
                decay_ref, skip_ref, residue_ref,
                out_ref, part_ref, gg_ref, sg_ref, acc_ref,
                sig, res, last, e_all, end_ref, recv_ref, rows_ref, scale_ref, came_ref,
                send_sem, recv_sem, row_send, row_recv, tile_sem):
    peers = recv_ref.shape[0] + 1
    mine = lax.axis_index("ctx")
    segment = lax.axis_index("pipe")
    chunk = sav_ref.shape[1]
    chunks = end_ref.shape[2] // chunk
    step = pl.program_id(0)
    sf_ref, sb_ref = scale_ref.at[0], scale_ref.at[1]
    length = sav_ref.shape[0]
    steps = length // ROWS
    modes = decay_ref.shape[0]

    def incoming(here):
        return rows_ref[1, :, here].astype(jnp.float32)

    def cotangent(here):
        return rows_ref[0, :, here].astype(jnp.float32)

    def move(c, forward):
        lanes = pl.ds(pl.multiple_of(c * chunk, chunk), chunk)
        target = jnp.minimum(segment + 1, segments - 1) if forward else jnp.maximum(segment - 1, 0)
        return pltpu.make_async_remote_copy(
            src_ref=bound_ref.at[0, forward, :, lanes],
            dst_ref=rows_ref.at[forward, :, lanes],
            send_sem=row_send.at[c, forward],
            recv_sem=row_recv.at[c, forward],
            device_id={"pipe": target},
            device_id_type=pl.DeviceIdType.MESH,
        )

    def move_tile():
        return pltpu.make_async_remote_copy(
            src_ref=square_ref.at[0],
            dst_ref=came_ref,
            send_sem=tile_sem.at[0],
            recv_sem=tile_sem.at[1],
            device_id={"pipe": jnp.minimum(segment + 1, segments - 1)},
            device_id_type=pl.DeviceIdType.MESH,
        )

    first = segment == 0
    final = segment == segments - 1

    def copy(c, far, rev):
        lanes = pl.ds(pl.multiple_of(c * chunk, chunk), chunk)
        parts = pl.ds(2, 1) if rev else pl.ds(0, 2)
        index = 2 * (far - 1) + rev
        return pltpu.make_async_remote_copy(
            src_ref=end_ref.at[parts, :, lanes],
            dst_ref=recv_ref.at[far - 1, parts, :, lanes],
            send_sem=send_sem.at[c, index],
            recv_sem=recv_sem.at[c, index],
            device_id={"ctx": jnp.maximum(mine - far, 0) if rev else jnp.minimum(mine + far, peers - 1)},
            device_id_type=pl.DeviceIdType.MESH,
        )

    @pl.when(step == 0)
    def _():
        barrier = pltpu.get_barrier_semaphore()
        for far in range(1, peers):
            pl.semaphore_signal(barrier, inc=1, device_id={"ctx": lax.rem(mine + far, peers)},
                                device_id_type=pl.DeviceIdType.MESH)

        @pl.when(jnp.logical_not(first))
        def _():
            pl.semaphore_signal(barrier, inc=1, device_id={"pipe": jnp.maximum(segment - 1, 0)},
                                device_id_type=pl.DeviceIdType.MESH)

        @pl.when(jnp.logical_not(final))
        def _():
            pl.semaphore_signal(barrier, inc=1,
                                device_id={"pipe": jnp.minimum(segment + 1, segments - 1)},
                                device_id_type=pl.DeviceIdType.MESH)

        around = jnp.where(first, 0, 1) + jnp.where(final, 0, 1)
        pl.semaphore_wait(barrier, peers - 1 + around)

        @pl.when(jnp.logical_not(final))
        def _():
            move_tile().start()

        for c in range(chunks):
            @pl.when(jnp.logical_not(final))
            def _():
                move(c, 1).start()

            @pl.when(jnp.logical_not(first))
            def _():
                move(c, 0).start()

        acc_ref[...] = jnp.zeros_like(acc_ref)
        scale_ref[1] = lax.rsqrt(square_ref[1] / D + epsilon)

        @pl.when(first)
        def _():
            scale_ref[0] = lax.rsqrt(square_ref[2] / D + epsilon)

        @pl.when(jnp.logical_not(first))
        def _():
            move_tile().wait_recv()
            scale_ref[0] = lax.rsqrt(came_ref[...] / D + epsilon)

        @pl.when(jnp.logical_not(final))
        def _():
            move_tile().wait_send()

    @pl.when(step < chunks)
    def _():
        block = pl.ds(pl.multiple_of(step * chunk, chunk), chunk)

        @pl.when(first)
        def _():
            rows_ref[1, :, block] = emb_ref[...]

        @pl.when(jnp.logical_not(first))
        def _():
            move(step, 1).wait_recv()

        @pl.when(final)
        def _():
            rows_ref[0, :, block] = loss_ref[...]

        @pl.when(jnp.logical_not(final))
        def _():
            move(step, 0).wait_recv()

        place = lax.broadcasted_iota(jnp.int32, (ROWS, LANES), 0)

        def group(g, carry):
            lanes = pl.ds(pl.multiple_of(g * LANES, LANES), LANES)
            here = pl.ds(pl.multiple_of(step * chunk + g * LANES, LANES), LANES)
            gain = gain_ref[:, lanes]
            back = sav_ref[:, lanes].astype(jnp.float32) * sb_ref[...] * gain
            sig[0] = incoming(here) * sf_ref[...] * gain
            sig[1] = back
            sig[2] = cotangent(here) * back
            damping = decay_ref[:, lanes]
            a_all = jnp.exp(-damping)
            stride_all = jnp.exp(-damping * float(steps))
            a = [wide(a_all[k:k + 1]) for k in range(modes)]
            for q in range(3):
                rev = q == 2
                order = range(steps - 1, -1, -1) if rev else range(steps)
                state = None
                for j in order:
                    piece = sig[q, pl.ds(j, ROWS, stride=steps), :]
                    if state is None:
                        state = [piece] * modes
                    else:
                        state = [a[k] * state[k] + piece for k in range(modes)]
                for k in range(modes):
                    power = wide(stride_all[k:k + 1])
                    total = state[k]
                    hop = 1
                    while hop < ROWS:
                        near = (place < ROWS - hop) if rev else (place >= hop)
                        moved = pltpu.roll(total, ROWS - hop if rev else hop, 0)
                        total = total + jnp.where(near, power * moved, 0.0)
                        power = power * power
                        hop *= 2
                    near = (place < ROWS - 1) if rev else (place >= 1)
                    moved = pltpu.roll(total, ROWS - 1 if rev else 1, 0)
                    e_all[q, k, :, here] = jnp.where(near, moved, 0.0)
                    edge = 0 if rev else ROWS - 1
                    last[k:k + 1, :] = total[edge:edge + 1, :]
                end_ref[q, :, here] = last[...].astype(end_ref.dtype)
            return carry

        lax.fori_loop(0, chunk // LANES, group, 0)

        for far in range(1, peers):
            @pl.when(mine + far < peers)
            def _():
                copy(step, far, 0).start()

            @pl.when(mine >= far)
            def _():
                copy(step, far, 1).start()

    @pl.when(step >= chunks)
    def _():
        place = lax.broadcasted_iota(jnp.int32, (ROWS, LANES), 0).astype(jnp.float32)

        c = step - chunks

        @pl.when(jnp.logical_not(final))
        def _():
            move(c, 1).wait_send()

        @pl.when(jnp.logical_not(first))
        def _():
            move(c, 0).wait_send()

        for far in range(1, peers):
            @pl.when(mine + far < peers)
            def _():
                copy(c, far, 0).wait_send()
                copy(c, far, 1).wait_recv()

            @pl.when(mine >= far)
            def _():
                copy(c, far, 1).wait_send()
                copy(c, far, 0).wait_recv()

        def group(g, carry):
            lanes = pl.ds(pl.multiple_of(g * LANES, LANES), LANES)
            here = pl.ds(pl.multiple_of(c * chunk + g * LANES, LANES), LANES)
            gain = gain_ref[:, lanes]
            gain_w = wide(gain)
            sig[0] = incoming(here)
            sig[1] = sav_ref[:, lanes].astype(jnp.float32) * sb_ref[...]
            sig[2] = cotangent(here)
            damping = decay_ref[:, lanes]
            a_all = jnp.exp(-damping)
            coefs = residue_ref[:, lanes] * jnp.sqrt(1.0 - jnp.exp(-2.0 * damping))
            whole = jnp.exp(-damping * float(length))
            entering = []
            for q in range(3):
                total = jnp.zeros((modes, LANES), jnp.float32)
                for far in range(peers - 1, 0, -1):
                    reached = (mine + far < peers) if q == 2 else (mine >= far)
                    longer = whole * total + recv_ref[far - 1, q, :, here].astype(jnp.float32)
                    total = jnp.where(reached, longer, total)
                entering.append(total)
            kernel = []
            power = coefs
            for n in range(steps):
                kernel.append(wide(jnp.sum(power, axis=0, keepdims=True)))
                power = power * a_all
            kernel[0] = kernel[0] + wide(skip_ref[:, lanes])

            def rows(i):
                return pl.ds(i, ROWS, stride=steps)

            def conv(q, pieces, emit):
                rev = q == 2
                near = []
                for n in range(steps):
                    near.append(summed([kernel[n - m] * pieces[steps - 1 - m if rev else m]
                                        for m in range(n + 1)]))
                ago = (float(ROWS - 1) - place) if rev else place
                decayed = []
                for k in range(modes):
                    gap = jnp.exp(wide(damping[k:k + 1]) * (ago * float(-steps)))
                    state = e_all[q, k, :, here] + gap * wide(entering[q][k:k + 1])
                    decayed.append(wide(coefs[k:k + 1]) * state)
                a = [wide(a_all[k:k + 1]) for k in range(modes)]
                for n in range(steps):
                    decayed = [a[k] * decayed[k] for k in range(modes)]
                    emit(steps - 1 - n if rev else n, summed([near[n]] + decayed))

            raw = [sig[0, rows(i), :] for i in range(steps)]
            normed = [raw[i] * sf_ref[rows(i), :] * gain_w for i in range(steps)]

            def emit_out(i, value):
                res[0, rows(i), :] = sig[0, rows(i), :] + sig[0, rows(i), :] * sf_ref[rows(i), :] * gain_w * value

            conv(0, normed, emit_out)
            out_ref[:, lanes] = res[0].astype(out_ref.dtype)

            back = [sig[1, rows(i), :] * gain_w for i in range(steps)]

            def emit_mixed(i, value):
                res[1, rows(i), :] = sig[2, rows(i), :] * value

            conv(1, back, emit_mixed)

            mix = [sig[2, rows(i), :] * back[i] for i in range(steps)]
            skip_sum = mix[0] * back[0]
            for i in range(1, steps):
                skip_sum = skip_sum + mix[i] * back[i]
            sg_ref[:, lanes] = skip_sum
            gain_sums = [jnp.zeros((ROWS, LANES), jnp.float32)]

            def emit_grad(i, value):
                norm = res[1, rows(i), :] + value
                unit = sig[1, rows(i), :]
                gain_sums[0] = gain_sums[0] + norm * unit
                scaled = gain_w * norm
                acc_ref[i] = acc_ref[i] + scaled * unit
                res[2, rows(i), :] = sig[2, rows(i), :] + sb_ref[rows(i), :] * scaled

            conv(2, mix, emit_grad)
            part_ref[:, lanes] = res[2]
            gg_ref[:, lanes] = gain_sums[0]
            return carry

        lax.fori_loop(0, chunk // LANES, group, 0)


def local(tokens, table, boundary, saved_in, loss_grad, gain, skip, residue, decay_rate):
    segments = lax.axis_size("pipe")
    onehot = (tokens[:, None] == jnp.arange(table.shape[0], dtype=jnp.int32)[None, :]).astype(
        jnp.bfloat16
    )
    embedded = jnp.dot(onehot, table, preferred_element_type=jnp.float32).astype(jnp.bfloat16)
    sav = saved_in[0]

    def squares_of(value):
        value = value.astype(jnp.float32)
        return jnp.sum(value * value, axis=1)

    squares = width_sum(
        jnp.stack([squares_of(boundary[0, 1]), squares_of(sav), squares_of(embedded)])
    )
    length, channels = sav.shape
    modes = decay_rate.shape[1]
    steps = length // ROWS
    squares_wide = jnp.broadcast_to(squares[:, :, None], (3, length, LANES))
    scale_back = lax.rsqrt(squares[1] / D + epsilon)
    chunk = min(CHUNK, channels)
    chunks = channels // chunk
    peers = lax.axis_size("ctx")
    f32 = jnp.float32
    work = length * channels

    def both(height):
        return pl.BlockSpec((height, chunk), lambda s: (0, lax.rem(s, chunks)))

    def early(height):
        return pl.BlockSpec((height, chunk), lambda s: (0, jnp.minimum(s, chunks - 1)))

    def late(height):
        return pl.BlockSpec((height, chunk), lambda s: (0, jnp.maximum(s - chunks, 0)))

    out, part, gain_grad, skip_grad, inner = pl.pallas_call(
        functools.partial(step_kernel, segments),
        grid=(2 * chunks,),
        in_specs=[
            pl.BlockSpec(memory_space=pl.ANY), early(length), both(length), early(length),
            pl.BlockSpec((3, length, LANES), lambda s: (0, 0, 0)),
            both(1), both(modes), late(1), late(modes),
        ],
        out_specs=[late(length), late(length), late(ROWS), late(ROWS),
                   pl.BlockSpec((steps, ROWS, LANES), lambda s: (0, 0, 0))],
        out_shape=[
            jax.ShapeDtypeStruct((length, channels), jnp.bfloat16),
            jax.ShapeDtypeStruct((length, channels), f32),
            jax.ShapeDtypeStruct((ROWS, channels), f32),
            jax.ShapeDtypeStruct((ROWS, channels), f32),
            jax.ShapeDtypeStruct((steps, ROWS, LANES), f32),
        ],
        scratch_shapes=[
            pltpu.VMEM((3, length, LANES), f32),
            pltpu.VMEM((3, length, LANES), f32),
            pltpu.VMEM((modes, LANES), f32),
            pltpu.VMEM((3, modes, ROWS, channels), f32),
            pltpu.VMEM((3, modes, channels), jnp.bfloat16),
            pltpu.VMEM((peers - 1, 3, modes, channels), jnp.bfloat16),
            pltpu.VMEM((2, length, channels), jnp.bfloat16),
            pltpu.VMEM((2, length, LANES), f32),
            pltpu.VMEM((length, LANES), f32),
            pltpu.SemaphoreType.DMA((chunks, 2 * (peers - 1))),
            pltpu.SemaphoreType.DMA((chunks, 2 * (peers - 1))),
            pltpu.SemaphoreType.DMA((chunks, 2)),
            pltpu.SemaphoreType.DMA((chunks, 2)),
            pltpu.SemaphoreType.DMA((2,)),
        ],
        compiler_params=pltpu.CompilerParams(
            vmem_limit_bytes=VMEM, collective_id=0, has_side_effects=True
        ),
        cost_estimate=pl.CostEstimate(flops=246 * work, bytes_accessed=26 * work, transcendentals=0),
    )(boundary, embedded, sav, loss_grad, squares_wide, gain, decay_rate[0], skip, residue[0])
    grads = [jnp.sum(rows, axis=0)[None, None, :] for rows in (gain_grad, skip_grad)]
    inner_sum = width_sum(jnp.sum(inner, axis=2)).T.reshape(length)
    factor = (scale_back ** 2 * inner_sum / D)[:, None]
    input_grad = (part - sav.astype(f32) * factor).astype(jnp.bfloat16)
    return (out[None], input_grad[None], grads[0], grads[1])


def solution(mesh):
    in_specs = (
        P("ctx"),
        P(None, "width"),
        P("pipe", None, "ctx", "width"),
        P("pipe", "ctx", "width"),
        P("ctx", "width"),
        P("pipe", "width"),
        P("pipe", "width"),
        P("pipe", None, "width"),
        P("pipe", None, "width"),
    )
    out_specs = (
        P("pipe", "ctx", "width"),
        P("pipe", "ctx", "width"),
        P("pipe", "ctx", "width"),
        P("pipe", "ctx", "width"),
    )
    return jax.shard_map(local, mesh=mesh, in_specs=in_specs, out_specs=out_specs, check_vma=False)
```
